256 devices in a mesh: frame: 128 (over y, x, z), tensor: 2 (over core).
Axes of the slice: x: 4, y: 4, z: 8, core: 2. Of those that a mesh axis runs over, the one named last changes fastest.
Arguments:
- queries: bfloat16 [65536, 3072], P('frame', 'tensor'), may hold values from -128 to 128
- context_keys: bfloat16 [1152, 3072], P(None, 'tensor'), may hold values from -8 to 8
- context_values: bfloat16 [1152, 3072], P(None, 'tensor'), may hold values from -6 to 6
- router_logit: float32 [65536], P('frame'), may hold values from -8 to 8
- keep_index: int32 [128, 512], P('frame'), may hold values from 0 to 512, as said below
- visible_blocks: int32 [128], P('frame'), may hold values from 1 to 9, as said below
- out_grad: bfloat16 [65536, 3072], P('frame', 'tensor'), may hold values from -12 to 12
Outputs:
- routed_out: bfloat16 [65536, 3072], P('frame', 'tensor')
- query_grad: bfloat16 [65536, 3072], P('frame', 'tensor')
- router_grad: float32 [65536], P('frame')
The draws below stay inside these ranges and needn't reach their ends.
Inputs may be any that keep to these rules, and one draw needn't show every extreme that they name: `keep_index`: row f lists the tokens of frame f that the routed layer keeps, in rising order, then 512 in every unused place. All rows together keep exactly 16384 tokens, every frame keeps at least one, and one frame keeps all 512. The tokens of frame f see the context rows of memory blocks 0 to visible_blocks[f] - 1, blocks of 128 rows. It never falls from one frame to the next; the first frame sees one block and the last all 9.
All inputs are finite; a program needn't handle non-finite values.
Results may differ from the reference program's by a relative error of at most 0.0064.
Values may be sent and summed in bfloat16 or wider, within the bound.
A program may use at most 128 MiB of HBM per device.

```python
import math
import jax
import jax.numpy as jnp
from jax import lax

TOK_DEV = 512
CTX = 1152
HEADS = 24
HD = 128
MEM_BLOCK = 128
FRAMES = 128
TOKENS = 65536
KEPT = 16384
MEM_BLOCKS = 9


def base_keys(key):
    return jnp.clip(jax.random.normal(jax.random.fold_in(key, 11), (CTX, HEADS * HD), jnp.float32), -5.0, 5.0)


def draw_context_keys(key, part):
    keys_base = base_keys(key)
    return keys_base.astype(jnp.bfloat16)


def draw_queries(key, part):
    key = jax.random.fold_in(key, 3)
    first_key = jax.random.fold_in(key, 0)
    result = 2.0 * jnp.clip(jax.random.normal(first_key, (TOKENS, HEADS * HD), jnp.float32), -6.0, 6.0)
    return result.astype(jnp.bfloat16)


def draw_keep_index(key, part):
    key = jax.random.fold_in(key, 5)
    first_key, second_key, third_key, fourth_key = jax.random.split(key, 4)
    full_frame = jax.random.randint(first_key, (), 0, FRAMES)
    ranking = jax.random.permutation(second_key, FRAMES - 1)
    weights = 1 + ranking % 5
    weight_total = jnp.sum(weights)
    remaining = KEPT - TOK_DEV
    shares = remaining * weights // weight_total
    short_by = remaining - jnp.sum(shares)
    extra_rank = jax.random.permutation(third_key, FRAMES - 1)
    shares = shares + (extra_rank < short_by).astype(jnp.int32)
    frame_ids = jnp.arange(FRAMES, dtype=jnp.int32)
    other_pos = jnp.clip(frame_ids - (frame_ids > full_frame).astype(jnp.int32), 0, FRAMES - 2)
    counts = jnp.where(frame_ids == full_frame, TOK_DEV, shares[other_pos]).astype(jnp.int32)
    token_ids = jnp.arange(TOK_DEV, dtype=jnp.int32)

    def one_frame(frame_number, frame_count):
        shuffle = jax.random.permutation(jax.random.fold_in(fourth_key, frame_number), TOK_DEV)
        chosen = shuffle < frame_count
        sort_keys = jnp.where(chosen, token_ids, TOK_DEV + token_ids)
        ordering = jnp.argsort(sort_keys, stable=True)
        return jnp.where(token_ids < frame_count, token_ids[ordering], TOK_DEV).astype(jnp.int32)
    return jax.vmap(one_frame)(frame_ids, counts)


def draw_visible_blocks(key, part):
    key = jax.random.fold_in(key, 7)
    raised = jnp.sort(jax.random.randint(key, (FRAMES,), 1, MEM_BLOCKS + 1))
    return raised.at[0].set(1).at[FRAMES - 1].set(MEM_BLOCKS).astype(jnp.int32)


def levels(key, dims, shards, smallest, high):
    level, own = 1.0, jax.random.fold_in(key, 6)
    for dim, parts in shards:
        steps = jnp.exp(jax.random.uniform(jax.random.fold_in(own, dim), (parts,), jnp.float32, smallest / len(shards), high / len(shards)))
        level = level * jnp.repeat(steps, dims[dim] // parts).reshape([-1 if axis == dim else 1 for axis in range(len(dims))])
    return level


def bell_draw(rng, shape, scale, limit, cuts=(), held_as=jnp.bfloat16):
    drawn = scale * jax.random.normal(rng, shape, jnp.float32)
    if cuts:
        drawn = drawn * levels(rng, shape, cuts, -0.22, 0.18)
    return jnp.clip(drawn, -limit, limit).astype(held_as)


def setup_inputs(seed: int = 0) -> dict:
    arg_keys = jax.random.split(jax.random.key(seed), 8)
    queries = draw_queries(jax.random.fold_in(arg_keys[7], 71), 0)
    context_keys = draw_context_keys(jax.random.fold_in(arg_keys[7], 71), 0)
    context_values = bell_draw(arg_keys[2], (CTX, HEADS * HD), 1.0, 6.0, ((1, 2),))
    router_logit = bell_draw(arg_keys[3], (TOKENS,), 2.0, 8.0, ((0, 128),), jnp.float32)
    keep_index = draw_keep_index(jax.random.fold_in(arg_keys[7], 71), 0)
    visible_blocks = draw_visible_blocks(jax.random.fold_in(arg_keys[7], 71), 0)
    out_grad = bell_draw(arg_keys[6], (TOKENS, HEADS * HD), 2.0, 12.0, ((0, 128), (1, 2)))
    return {"queries": queries, "context_keys": context_keys, "context_values": context_values, "router_logit": router_logit, "keep_index": keep_index, "visible_blocks": visible_blocks, "out_grad": out_grad}


def reference(queries, context_keys, context_values, router_logit, keep_index, visible_blocks, out_grad):
    feat_width = HEADS * HD
    scale = HD ** -0.5
    frame_base = jnp.arange(FRAMES, dtype=jnp.int32)[:, None] * TOK_DEV
    flat_tokens = (frame_base + keep_index).reshape(-1)
    flat_valid = (keep_index < TOK_DEV).reshape(-1)
    picked = jnp.nonzero(flat_valid, size=KEPT)[0].astype(jnp.int32)
    token_ids = flat_tokens[picked].astype(jnp.int32)
    frame_ids = (picked // TOK_DEV).astype(jnp.int32)
    gate_value = jax.nn.sigmoid(router_logit)
    grad_attn = (gate_value[:, None] * out_grad.astype(jnp.float32)).astype(jnp.bfloat16)
    keys_heads = context_keys.astype(jnp.float32).reshape(CTX, HEADS, HD)
    values_heads = context_values.astype(jnp.float32).reshape(CTX, HEADS, HD)
    block_rows = math.gcd(KEPT, 512)
    block_count = KEPT // block_rows
    token_blocks = token_ids.reshape(block_count, block_rows)
    limit_blocks = visible_blocks[frame_ids].astype(jnp.int32).reshape(block_count, block_rows)
    block_of = jnp.arange(CTX, dtype=jnp.int32) // MEM_BLOCK

    def one_block(carry, block):
        token_block, limit_block = block
        q_heads = queries[token_block].astype(jnp.float32).reshape(block_rows, HEADS, HD)
        g_heads = grad_attn[token_block].astype(jnp.float32).reshape(block_rows, HEADS, HD)
        scores = jnp.einsum("rhd,chd->rhc", q_heads, keys_heads) * scale
        scores = jnp.where(block_of[None, None, :] < limit_block[:, None, None], scores, -jnp.inf)
        row_top = jnp.max(scores, axis=2, keepdims=True)
        exp_terms = jnp.exp(scores - row_top)
        exp_total = jnp.sum(exp_terms, axis=2, keepdims=True)
        prob_rows = lax.optimization_barrier((exp_terms / exp_total).astype(jnp.bfloat16)).astype(jnp.float32)
        mixed_rows = jnp.einsum("rhc,chd->rhd", prob_rows, values_heads)
        attn_rows = mixed_rows.astype(jnp.bfloat16).reshape(block_rows, feat_width)
        log_total = row_top + jnp.log(exp_total)
        delta_rows = jnp.sum(g_heads * mixed_rows, axis=2, keepdims=True)
        back_probs = jnp.exp(scores - log_total)
        dprob_rows = jnp.einsum("rhd,chd->rhc", g_heads, values_heads)
        dscore_rows = lax.optimization_barrier((back_probs * (dprob_rows - delta_rows)).astype(jnp.bfloat16)).astype(jnp.float32)
        query_part = (jnp.einsum("rhc,chd->rhd", dscore_rows, keys_heads) * scale).astype(jnp.bfloat16).reshape(block_rows, feat_width)
        return carry, (attn_rows, query_part)

    _, (attn_all, query_all) = lax.scan(one_block, jnp.zeros((), jnp.float32), (token_blocks, limit_blocks))
    attn_tok = jnp.zeros((TOKENS, feat_width), jnp.bfloat16).at[token_ids].set(attn_all.reshape(KEPT, feat_width))
    query_grad = jnp.zeros((TOKENS, feat_width), jnp.bfloat16).at[token_ids].set(query_all.reshape(KEPT, feat_width))
    routed_out = (gate_value[:, None] * attn_tok.astype(jnp.float32)).astype(jnp.bfloat16)
    inner = jnp.sum(out_grad.astype(jnp.float32) * attn_tok.astype(jnp.float32), axis=1)
    router_grad = gate_value * (1.0 - gate_value) * inner
    return routed_out, query_grad, router_grad
```

```python
import functools

import jax
import jax.numpy as jnp
from jax import lax
from jax.experimental import pallas as pl
from jax.experimental.pallas import tpu as pltpu
from jax.sharding import PartitionSpec as P

HD = 128
MEM_BLOCK = 128
SCALE = HD ** (-0.5)
LOG2E = 1.4426950408889634
PAIR = 2
ROWS = 128

NT = (((1,), (1,)), ((), ()))


def dot(a, b):
    return jnp.dot(a, b, preferred_element_type=jnp.float32)


def dot_nt(a, b):
    return lax.dot_general(a, b, NT, preferred_element_type=jnp.float32)


def attend(q, g, keys, values):
    scores = dot_nt(q, keys)
    top = jnp.max(scores, axis=1, keepdims=True)
    terms = jnp.exp2((scores - top) * (SCALE * LOG2E))
    ones = jnp.ones(values.shape, values.dtype)
    sums = dot(terms.astype(jnp.bfloat16), jnp.concatenate([values, ones], axis=1))
    inverse = 1.0 / sums[:, HD:]
    mixed = sums[:, :HD] * inverse
    delta = jnp.sum(g.astype(jnp.float32) * mixed, axis=1, keepdims=True)
    dprob = dot_nt(g, values)
    dscore = (terms * (dprob - delta)).astype(jnp.bfloat16)
    dq = dot(dscore, keys) * (inverse * SCALE)
    return mixed.astype(jnp.bfloat16), dq.astype(jnp.bfloat16)


def kernel(
    visible_ref, keep_ref, logit_ref, q_ref, k_ref, v_ref, og_ref,
    out_ref, dq_ref, part_ref,
    gate, pick, place, qc, gc, ac, dc, acc, count_ref,
):
    tokens = q_ref.shape[0]
    blocks = k_ref.shape[0] // MEM_BLOCK
    step = pl.program_id(0)

    @pl.when(step == 0)
    def _():
        keep = keep_ref[...]
        count_ref[0] = jnp.sum((keep < tokens).astype(jnp.int32))
        spread = jnp.broadcast_to(logit_ref[...], (HD, tokens))
        gate[...] = jax.nn.sigmoid(jnp.transpose(spread))
        acc[...] = jnp.zeros_like(acc)
        token = lax.broadcasted_iota(jnp.int32, (tokens, tokens), 0)
        onehot = jnp.where(token == keep, 1.0, 0.0)
        place[...] = onehot.astype(jnp.bfloat16)
        pick[...] = jnp.transpose(onehot).astype(jnp.bfloat16)
        ac[...] = jnp.zeros_like(ac)
        dc[...] = jnp.zeros_like(dc)

    count = count_ref[0]
    full = count == tokens
    g_all = gate[...]
    gated = jnp.concatenate(
        [
            (g_all * og_ref[:, h * HD : (h + 1) * HD].astype(jnp.float32)).astype(jnp.bfloat16)
            for h in range(PAIR)
        ],
        axis=1,
    )

    @pl.when(full)
    def _():
        qc[...] = q_ref[...]
        gc[...] = gated

    @pl.when(jnp.logical_not(full))
    def _():
        qc[...] = dot(pick[...], q_ref[...]).astype(jnp.bfloat16)
        gc[...] = dot(pick[...], gated).astype(jnp.bfloat16)

    tiles = (count + (ROWS - 1)) // ROWS
    visible = visible_ref[0]
    for reach in range(1, blocks + 1):

        @pl.when(visible == reach)
        def _():
            span = reach * MEM_BLOCK

            @pl.loop(0, tiles)
            def _(tile):
                rows = pl.ds(pl.multiple_of(tile * ROWS, ROWS), ROWS)
                for h in range(PAIR):
                    cols = slice(h * HD, (h + 1) * HD)
                    mixed, dq = attend(
                        qc[rows, cols], gc[rows, cols], k_ref[:span, cols], v_ref[:span, cols]
                    )
                    ac[rows, cols] = mixed
                    dc[rows, cols] = dq

    def finish(attn):
        total = acc[...]
        for h in range(PAIR):
            cols = slice(h * HD, (h + 1) * HD)
            part = attn[:, cols].astype(jnp.float32)
            out_ref[:, cols] = (g_all * part).astype(jnp.bfloat16)
            total = total + og_ref[:, cols].astype(jnp.float32) * part
        acc[...] = total

    @pl.when(full)
    def _():
        finish(ac[...])
        dq_ref[...] = dc[...]

    @pl.when(jnp.logical_not(full))
    def _():
        finish(dot(place[...], ac[...]).astype(jnp.bfloat16))
        dq_ref[...] = dot(place[...], dc[...]).astype(jnp.bfloat16)

    @pl.when(step == pl.num_programs(0) - 1)
    def _():
        turned = jnp.transpose(acc[...])
        gated_row = jax.nn.sigmoid(logit_ref[...])
        part_ref[...] = jnp.sum(turned, axis=0, keepdims=True) * (gated_row * (1.0 - gated_row))


def local(queries, keys, values, logit, keep, visible, out_grad):
    tokens, width = queries.shape
    ctx = keys.shape[0]
    wide = PAIR * HD
    column = lambda rows: pl.BlockSpec((rows, wide), lambda s: (0, s))
    whole = pl.BlockSpec((1, tokens), lambda s: (0, 0))
    return pl.pallas_call(
        kernel,
        grid=(width // wide,),
        in_specs=[
            pl.BlockSpec(memory_space=pltpu.SMEM),
            whole,
            whole,
            column(tokens),
            column(ctx),
            column(ctx),
            column(tokens),
        ],
        out_specs=[column(tokens), column(tokens), whole],
        out_shape=[
            jax.ShapeDtypeStruct((tokens, width), jnp.bfloat16),
            jax.ShapeDtypeStruct((tokens, width), jnp.bfloat16),
            jax.ShapeDtypeStruct((1, tokens), jnp.float32),
        ],
        scratch_shapes=[
            pltpu.VMEM((tokens, HD), jnp.float32),
            pltpu.VMEM((tokens, tokens), jnp.bfloat16),
            pltpu.VMEM((tokens, tokens), jnp.bfloat16),
            pltpu.VMEM((tokens, wide), jnp.bfloat16),
            pltpu.VMEM((tokens, wide), jnp.bfloat16),
            pltpu.VMEM((tokens, wide), jnp.bfloat16),
            pltpu.VMEM((tokens, wide), jnp.bfloat16),
            pltpu.VMEM((tokens, HD), jnp.float32),
            pltpu.SMEM((1,), jnp.int32),
        ],
        compiler_params=pltpu.CompilerParams(
            dimension_semantics=("arbitrary",), vmem_limit_bytes=48 * 1024 * 1024
        ),
    )(visible, keep, logit.reshape(1, tokens), queries, keys, values, out_grad)


def per_device(queries, context_keys, context_values, router_logit, keep_index, visible_blocks, out_grad):
    routed_out, query_grad, part = local(
        queries, context_keys, context_values, router_logit, keep_index, visible_blocks, out_grad
    )
    router_grad = lax.psum(part.reshape(-1), "tensor")
    return routed_out, query_grad, router_grad


def solution(mesh):
    return jax.shard_map(
        per_device,
        mesh=mesh,
        in_specs=(
            P("frame", "tensor"),
            P(None, "tensor"),
            P(None, "tensor"),
            P("frame"),
            P("frame", None),
            P("frame"),
            P("frame", "tensor"),
        ),
        out_specs=(P("frame", "tensor"), P("frame", "tensor"), P("frame")),
        check_vma=False,
    )
```

```python
import jax
import jax.numpy as jnp
from jax import lax
from jax.experimental import pallas as pl
from jax.experimental.pallas import tpu as pltpu
from jax.sharding import PartitionSpec as P

HD = 128
MEM_BLOCK = 128
SCALE = HD ** (-0.5)
LOG2E = 1.4426950408889634
UNIT = 2
FEW_UNITS = 2
ROWS = 256
FEW = 224
AHEAD = 2
MANY_REACH = (4, 5, 6, 7, 8, 9)
FEW_REACH = (8, 9)


def dot(a, b):
    return jnp.dot(a, b, preferred_element_type=jnp.float32)


def dot_nt(a, b):
    return lax.dot_general(a, b, (((1,), (1,)), ((), ())), preferred_element_type=jnp.float32)


def half(a):
    return a.astype(jnp.bfloat16)


def attend(q, g, keys, values, hidden):
    heads = range(len(q))
    scores = [dot_nt(q[h], keys[h]) for h in heads]
    dprob = [dot_nt(g[h], values[h]) for h in heads]
    if hidden is not None:
        scores = [hidden(s) for s in scores]
    top = [jnp.max(scores[h], axis=1, keepdims=True) for h in heads]
    terms = [jnp.exp2((scores[h] - top[h]) * (SCALE * LOG2E)) for h in heads]
    ones = jnp.ones(values[0].shape, values[0].dtype)
    sums = [dot(half(terms[h]), jnp.concatenate([values[h], ones], axis=1)) for h in heads]
    inverse = [1.0 / sums[h][:, HD:] for h in heads]
    mixed = [sums[h][:, :HD] * inverse[h] for h in heads]
    delta = [jnp.sum(g[h].astype(jnp.float32) * mixed[h], axis=1, keepdims=True) for h in heads]
    dscore = [half(terms[h] * (dprob[h] - delta[h])) for h in heads]
    dq = [dot(dscore[h], keys[h]) * (inverse[h] * SCALE) for h in heads]
    return [half(m).astype(jnp.float32) for m in mixed], [half(d) for d in dq]


def kernel(
    visible_hbm, keep_hbm, logit_hbm, q_hbm, k_hbm, v_hbm, og_hbm,
    out_hbm, dq_hbm, part_hbm,
    visible, keep_scalar, keep, logit, q_all, k_all, v_all, og_all, out_all, dq_all, part,
    gate, pick, place, acc, small_sem, in_sem, out_sem,
):
    tokens, width = q_all.shape
    unit = UNIT * HD
    groups = width // unit

    def columns(group, units=1):
        return pl.ds(pl.multiple_of(group * unit, unit), units * unit)

    def loads(group):
        cols = columns(group)
        pairs = ((q_hbm, q_all), (k_hbm, k_all), (og_hbm, og_all), (v_hbm, v_all))
        return [
            pltpu.make_async_copy(src.at[:, cols], dst.at[:, cols], in_sem.at[i, group])
            for i, (src, dst) in enumerate(pairs)
        ]

    def stores(group):
        cols = columns(group)
        pairs = ((out_all, out_hbm), (dq_all, dq_hbm))
        return [
            pltpu.make_async_copy(src.at[:, cols], dst.at[:, cols], out_sem.at[i, group])
            for i, (src, dst) in enumerate(pairs)
        ]

    small = [
        pltpu.make_async_copy(src, dst, small_sem.at[i])
        for i, (src, dst) in enumerate(
            ((visible_hbm, visible), (keep_hbm, keep_scalar), (keep_hbm, keep), (logit_hbm, logit))
        )
    ]
    for copy in small:
        copy.start()
    for group in range(AHEAD):
        for copy in loads(group):
            copy.start()
    for copy in small:
        copy.wait()

    gate_row = jax.nn.sigmoid(logit[...])
    gate[...] = jnp.transpose(jnp.broadcast_to(gate_row, (HD, tokens)))
    acc[...] = jnp.zeros_like(acc)
    shown = visible[0]
    full = keep_scalar[0, tokens - 1] < tokens
    few = keep_scalar[0, FEW] >= tokens
    some = jnp.logical_not(full)
    many = jnp.logical_not(few)

    @pl.when(some)
    def _():
        kept = keep[...]
        token = lax.broadcasted_iota(jnp.int32, (tokens, tokens), 0)
        place[...] = half(jnp.where(token == kept, 1.0, 0.0))
        spread = jnp.transpose(jnp.broadcast_to(kept.astype(jnp.float32), (HD, tokens)))
        lane = lax.broadcasted_iota(jnp.int32, (tokens, HD), 1).astype(jnp.float32)
        own = jnp.zeros((tokens, HD), jnp.float32)
        for start in range(0, tokens, HD):
            hit = jnp.where(spread == lane + float(start), 1.0, 0.0)
            pick[:, start : start + HD] = half(hit)
            own = own + hit * gate_row[:, start : start + HD]
        gate[...] = jnp.broadcast_to(jnp.sum(own, axis=1, keepdims=True), (tokens, HD))

    def sweep(units, body):
        @pl.loop(0, groups // units)
        def _(index):
            first = index * units
            for part_of in range(units):
                for copy in loads(first + part_of):
                    copy.wait()

            @pl.when(first + AHEAD < groups)
            def _():
                for part_of in range(units):
                    for copy in loads(first + AHEAD + part_of):
                        copy.start()

            body(first)
            for part_of in range(units):
                for copy in stores(first + part_of):
                    copy.start()

    def head_columns(group, units=1):
        return [
            pl.ds(pl.multiple_of(group * unit + h * HD, HD), HD) for h in range(units * UNIT)
        ]

    def hide(span, exact):
        if exact:
            return None

        def hidden(scores):
            col = lax.broadcasted_iota(jnp.int32, scores.shape, 1)
            return jnp.where(col < shown * MEM_BLOCK, scores, -jnp.inf)

        return hidden

    def tile(span, exact, cols, q, og, gates):
        g = [half(gates * o) for o in og]
        attn, dq = attend(
            q, g, [k_all[:span, c] for c in cols], [v_all[:span, c] for c in cols], hide(span, exact)
        )
        inner = og[0] * attn[0]
        for o, a in zip(og[1:], attn[1:]):
            inner = inner + o * a
        return [half(gates * a) for a in attn], dq, inner

    def run_many(span, exact, group):
        wide_cols = columns(group)
        cols = head_columns(group)

        @pl.when(some)
        def _():
            q_all[:, wide_cols] = half(dot(pick[...], q_all[:, wide_cols]))
            og_all[:, wide_cols] = half(dot(pick[...], og_all[:, wide_cols]))

        routed, dq, inner = tile(
            span, exact, cols,
            [q_all[:, c] for c in cols],
            [og_all[:, c].astype(jnp.float32) for c in cols],
            gate[...],
        )
        for h, c in enumerate(cols):
            out_all[:, c] = routed[h]
            dq_all[:, c] = dq[h]
        acc[...] = acc[...] + inner

        @pl.when(some)
        def _():
            out_all[:, wide_cols] = half(dot(place[...], out_all[:, wide_cols]))
            dq_all[:, wide_cols] = half(dot(place[...], dq_all[:, wide_cols]))

    def run_few(span, exact, group):
        wide_cols = columns(group, FEW_UNITS)
        cols = head_columns(group, FEW_UNITS)
        chosen = pick[:FEW, :]
        q = half(dot(chosen, q_all[:, wide_cols]))
        og = dot(chosen, og_all[:, wide_cols])
        routed, dq, inner = tile(
            span, exact, cols,
            [q[:, h * HD : (h + 1) * HD] for h in range(len(cols))],
            [og[:, h * HD : (h + 1) * HD] for h in range(len(cols))],
            gate[:FEW, :],
        )
        acc[:FEW, :] = acc[:FEW, :] + inner
        blank = jnp.zeros((ROWS - FEW, FEW_UNITS * unit), jnp.bfloat16)
        for target, rows in ((out_all, routed), (dq_all, dq)):
            stacked = jnp.concatenate([jnp.concatenate(rows, axis=1), blank], axis=0)
            target[:, wide_cols] = half(dot(place[:, :ROWS], stacked))

    def choose(reaches, run, wanted, units):
        low = 0
        for reach in reaches:
            span, exact = reach * MEM_BLOCK, reach == low + 1
            here = jnp.logical_and(shown > low, shown <= reach)

            @pl.when(jnp.logical_and(here, wanted))
            def _():
                sweep(units, lambda group: run(span, exact, group))

            low = reach

    choose(FEW_REACH, run_few, few, FEW_UNITS)
    choose(MANY_REACH, run_many, many, 1)

    weight = gate_row * (1.0 - gate_row)

    @pl.when(full)
    def _():
        part[...] = jnp.sum(jnp.transpose(acc[...]), axis=0, keepdims=True) * weight

    @pl.when(some)
    def _():
        inner = jnp.sum(acc[...], axis=1, keepdims=True)
        part[...] = jnp.sum(pick[...].astype(jnp.float32) * inner, axis=0, keepdims=True) * weight

    last = pltpu.make_async_copy(part, part_hbm, small_sem.at[0])
    last.start()
    for group in range(groups):
        for copy in stores(group):
            copy.wait()
    last.wait()


def local(queries, keys, values, logit, keep, visible, out_grad):
    tokens, width = queries.shape
    ctx = keys.shape[0]
    groups = width // (UNIT * HD)
    hbm = pl.BlockSpec(memory_space=pl.ANY)
    return pl.pallas_call(
        kernel,
        in_specs=[hbm] * 7,
        out_specs=[hbm] * 3,
        out_shape=[
            jax.ShapeDtypeStruct((tokens, width), jnp.bfloat16),
            jax.ShapeDtypeStruct((tokens, width), jnp.bfloat16),
            jax.ShapeDtypeStruct((1, tokens), jnp.float32),
        ],
        scratch_shapes=[
            pltpu.SMEM((1,), jnp.int32),
            pltpu.SMEM((1, tokens), jnp.int32),
            pltpu.VMEM((1, tokens), jnp.int32),
            pltpu.VMEM((1, tokens), jnp.float32),
            pltpu.VMEM((tokens, width), jnp.bfloat16),
            pltpu.VMEM((ctx, width), jnp.bfloat16),
            pltpu.VMEM((ctx, width), jnp.bfloat16),
            pltpu.VMEM((tokens, width), jnp.bfloat16),
            pltpu.VMEM((tokens, width), jnp.bfloat16),
            pltpu.VMEM((tokens, width), jnp.bfloat16),
            pltpu.VMEM((1, tokens), jnp.float32),
            pltpu.VMEM((tokens, HD), jnp.float32),
            pltpu.VMEM((tokens, tokens), jnp.bfloat16),
            pltpu.VMEM((tokens, tokens), jnp.bfloat16),
            pltpu.VMEM((tokens, HD), jnp.float32),
            pltpu.SemaphoreType.DMA((4,)),
            pltpu.SemaphoreType.DMA((4, groups)),
            pltpu.SemaphoreType.DMA((2, groups)),
        ],
        compiler_params=pltpu.CompilerParams(vmem_limit_bytes=60 * 1024 * 1024),
    )(visible, keep, logit.reshape(1, tokens), queries, keys, values, out_grad)


def per_device(queries, context_keys, context_values, router_logit, keep_index, visible_blocks, out_grad):
    routed_out, query_grad, part = local(
        queries, context_keys, context_values, router_logit, keep_index, visible_blocks, out_grad
    )
    router_grad = lax.psum(part.reshape(-1), "tensor")
    return routed_out, query_grad, router_grad


def solution(mesh):
    return jax.shard_map(
        per_device,
        mesh=mesh,
        in_specs=(
            P("frame", "tensor"),
            P(None, "tensor"),
            P(None, "tensor"),
            P("frame"),
            P("frame", None),
            P("frame"),
            P("frame", "tensor"),
        ),
        out_specs=(P("frame", "tensor"), P("frame", "tensor"), P("frame")),
        check_vma=False,
    )
```

```python
import jax
import jax.numpy as jnp
from jax import lax
from jax.experimental import pallas as pl
from jax.experimental.pallas import tpu as pltpu
from jax.sharding import PartitionSpec as P

HD = 128
MEM_BLOCK = 128
SCALE = HD ** (-0.5)
LOG2E = 1.4426950408889634
UNIT = 2
FEW_UNITS = 2
ROWS = 256
FEW = 224
AHEAD = 2
MANY_REACH = (4, 5, 6, 7, 8, 9)
FEW_REACH = (2, 8, 9)


def dot(a, b):
    return jnp.dot(a, b, preferred_element_type=jnp.float32)


def dot_nt(a, b):
    return lax.dot_general(a, b, (((1,), (1,)), ((), ())), preferred_element_type=jnp.float32)


def half(a):
    return a.astype(jnp.bfloat16)


def attend(q, g, keys, values, hidden):
    heads = range(len(q))
    scores = [dot_nt(q[h], keys[h]) for h in heads]
    dprob = [dot_nt(g[h], values[h]) for h in heads]
    if hidden is not None:
        scores = [hidden(s) for s in scores]
    top = [jnp.max(scores[h], axis=1, keepdims=True) for h in heads]
    terms = [jnp.exp2((scores[h] - top[h]) * (SCALE * LOG2E)) for h in heads]
    ones = jnp.ones(values[0].shape, values[0].dtype)
    sums = [dot(half(terms[h]), jnp.concatenate([values[h], ones], axis=1)) for h in heads]
    inverse = [1.0 / sums[h][:, HD:] for h in heads]
    mixed = [sums[h][:, :HD] * inverse[h] for h in heads]
    delta = [jnp.sum(g[h].astype(jnp.float32) * mixed[h], axis=1, keepdims=True) for h in heads]
    dscore = [half(terms[h] * (dprob[h] - delta[h])) for h in heads]
    dq = [dot(dscore[h], keys[h]) * (inverse[h] * SCALE) for h in heads]
    return [half(m).astype(jnp.float32) for m in mixed], [half(d) for d in dq]


def kernel(
    visible_hbm, keep_hbm, logit_hbm, q_hbm, k_hbm, v_hbm, og_hbm,
    out_hbm, dq_hbm, part_hbm,
    visible, keep_scalar, keep, logit, q_all, k_all, v_all, og_all, out_all, dq_all, part,
    gate, pick, place, acc, small_sem, in_sem, out_sem,
):
    tokens, width = q_all.shape
    unit = UNIT * HD
    groups = width // unit

    def columns(group, units=1):
        return pl.ds(pl.multiple_of(group * unit, unit), units * unit)

    def loads(group):
        cols = columns(group)
        pairs = ((q_hbm, q_all), (k_hbm, k_all), (og_hbm, og_all), (v_hbm, v_all))
        return [
            pltpu.make_async_copy(src.at[:, cols], dst.at[:, cols], in_sem.at[i, group])
            for i, (src, dst) in enumerate(pairs)
        ]

    def stores(group):
        cols = columns(group)
        pairs = ((out_all, out_hbm), (dq_all, dq_hbm))
        return [
            pltpu.make_async_copy(src.at[:, cols], dst.at[:, cols], out_sem.at[i, group])
            for i, (src, dst) in enumerate(pairs)
        ]

    small = [
        pltpu.make_async_copy(src, dst, small_sem.at[i])
        for i, (src, dst) in enumerate(
            ((visible_hbm, visible), (keep_hbm, keep_scalar), (keep_hbm, keep), (logit_hbm, logit))
        )
    ]
    for copy in small:
        copy.start()
    for group in range(AHEAD):
        for copy in loads(group):
            copy.start()
    for copy in small:
        copy.wait()

    gate_row = jax.nn.sigmoid(logit[...])
    gate[...] = jnp.transpose(jnp.broadcast_to(gate_row, (HD, tokens)))
    acc[...] = jnp.zeros_like(acc)
    shown = visible[0]
    full = keep_scalar[0, tokens - 1] < tokens
    few = keep_scalar[0, FEW] >= tokens
    some = jnp.logical_not(full)
    many = jnp.logical_not(few)

    @pl.when(some)
    def _():
        kept = keep[...]
        token = lax.broadcasted_iota(jnp.int32, (tokens, tokens), 0)
        place[...] = half(jnp.where(token == kept, 1.0, 0.0))
        spread = jnp.transpose(jnp.broadcast_to(kept.astype(jnp.float32), (HD, tokens)))
        lane = lax.broadcasted_iota(jnp.int32, (tokens, HD), 1).astype(jnp.float32)
        own = jnp.zeros((tokens, HD), jnp.float32)
        for start in range(0, tokens, HD):
            hit = jnp.where(spread == lane + float(start), 1.0, 0.0)
            pick[:, start : start + HD] = half(hit)
            own = own + hit * gate_row[:, start : start + HD]
        gate[...] = jnp.broadcast_to(jnp.sum(own, axis=1, keepdims=True), (tokens, HD))

    def sweep(units, body):
        @pl.loop(0, groups // units)
        def _(index):
            first = index * units
            for part_of in range(units):
                for copy in loads(first + part_of):
                    copy.wait()

            @pl.when(first + AHEAD < groups)
            def _():
                for part_of in range(units):
                    for copy in loads(first + AHEAD + part_of):
                        copy.start()

            body(first)
            for part_of in range(units):
                for copy in stores(first + part_of):
                    copy.start()

    def head_columns(group, units=1):
        return [
            pl.ds(pl.multiple_of(group * unit + h * HD, HD), HD) for h in range(units * UNIT)
        ]

    def hide(span, exact):
        if exact:
            return None

        def hidden(scores):
            col = lax.broadcasted_iota(jnp.int32, scores.shape, 1)
            return jnp.where(col < shown * MEM_BLOCK, scores, -jnp.inf)

        return hidden

    def tile(span, exact, cols, q, og, gates):
        g = [half(gates * o) for o in og]
        attn, dq = attend(
            q, g, [k_all[:span, c] for c in cols], [v_all[:span, c] for c in cols], hide(span, exact)
        )
        inner = og[0] * attn[0]
        for o, a in zip(og[1:], attn[1:]):
            inner = inner + o * a
        return [half(gates * a) for a in attn], dq, inner

    def run_many(span, exact, group):
        wide_cols = columns(group)
        cols = head_columns(group)

        @pl.when(some)
        def _():
            q_all[:, wide_cols] = half(dot(pick[...], q_all[:, wide_cols]))
            og_all[:, wide_cols] = half(dot(pick[...], og_all[:, wide_cols]))

        routed, dq, inner = tile(
            span, exact, cols,
            [q_all[:, c] for c in cols],
            [og_all[:, c].astype(jnp.float32) for c in cols],
            gate[...],
        )
        for h, c in enumerate(cols):
            out_all[:, c] = routed[h]
            dq_all[:, c] = dq[h]
        acc[...] = acc[...] + inner

        @pl.when(some)
        def _():
            out_all[:, wide_cols] = half(dot(place[...], out_all[:, wide_cols]))
            dq_all[:, wide_cols] = half(dot(place[...], dq_all[:, wide_cols]))

    def run_few(span, exact, group):
        wide_cols = columns(group, FEW_UNITS)
        cols = head_columns(group, FEW_UNITS)
        chosen = pick[:FEW, :]
        q = half(dot(chosen, q_all[:, wide_cols]))
        og = dot(chosen, og_all[:, wide_cols])
        routed, dq, inner = tile(
            span, exact, cols,
            [q[:, h * HD : (h + 1) * HD] for h in range(len(cols))],
            [og[:, h * HD : (h + 1) * HD] for h in range(len(cols))],
            gate[:FEW, :],
        )
        acc[:FEW, :] = acc[:FEW, :] + inner
        blank = jnp.zeros((ROWS - FEW, FEW_UNITS * unit), jnp.bfloat16)
        for target, rows in ((out_all, routed), (dq_all, dq)):
            stacked = jnp.concatenate([jnp.concatenate(rows, axis=1), blank], axis=0)
            target[:, wide_cols] = half(dot(place[:, :ROWS], stacked))

    def choose(reaches, run, units):
        reach, low = reaches[-1], (0, *reaches)[-2]
        span, exact = reach * MEM_BLOCK, reach == low + 1

        def here():
            sweep(units, lambda group: run(span, exact, group))

        if low:
            lax.cond(shown > low, here, lambda: choose(reaches[:-1], run, units))
        else:
            here()

    lax.cond(
        few,
        lambda: choose(FEW_REACH, run_few, FEW_UNITS),
        lambda: choose(MANY_REACH, run_many, 1),
    )

    weight = gate_row * (1.0 - gate_row)

    @pl.when(full)
    def _():
        part[...] = jnp.sum(jnp.transpose(acc[...]), axis=0, keepdims=True) * weight

    @pl.when(some)
    def _():
        inner = jnp.sum(acc[...], axis=1, keepdims=True)
        part[...] = jnp.sum(pick[...].astype(jnp.float32) * inner, axis=0, keepdims=True) * weight

    last = pltpu.make_async_copy(part, part_hbm, small_sem.at[0])
    last.start()
    for group in range(groups):
        for copy in stores(group):
            copy.wait()
    last.wait()


def local(queries, keys, values, logit, keep, visible, out_grad):
    tokens, width = queries.shape
    ctx = keys.shape[0]
    groups = width // (UNIT * HD)
    hbm = pl.BlockSpec(memory_space=pl.ANY)
    return pl.pallas_call(
        kernel,
        in_specs=[hbm] * 7,
        out_specs=[hbm] * 3,
        out_shape=[
            jax.ShapeDtypeStruct((tokens, width), jnp.bfloat16),
            jax.ShapeDtypeStruct((tokens, width), jnp.bfloat16),
            jax.ShapeDtypeStruct((1, tokens), jnp.float32),
        ],
        scratch_shapes=[
            pltpu.SMEM((1,), jnp.int32),
            pltpu.SMEM((1, tokens), jnp.int32),
            pltpu.VMEM((1, tokens), jnp.int32),
            pltpu.VMEM((1, tokens), jnp.float32),
            pltpu.VMEM((tokens, width), jnp.bfloat16),
            pltpu.VMEM((ctx, width), jnp.bfloat16),
            pltpu.VMEM((ctx, width), jnp.bfloat16),
            pltpu.VMEM((tokens, width), jnp.bfloat16),
            pltpu.VMEM((tokens, width), jnp.bfloat16),
            pltpu.VMEM((tokens, width), jnp.bfloat16),
            pltpu.VMEM((1, tokens), jnp.float32),
            pltpu.VMEM((tokens, HD), jnp.float32),
            pltpu.VMEM((tokens, tokens), jnp.bfloat16),
            pltpu.VMEM((tokens, tokens), jnp.bfloat16),
            pltpu.VMEM((tokens, HD), jnp.float32),
            pltpu.SemaphoreType.DMA((4,)),
            pltpu.SemaphoreType.DMA((4, groups)),
            pltpu.SemaphoreType.DMA((2, groups)),
        ],
        compiler_params=pltpu.CompilerParams(vmem_limit_bytes=60 * 1024 * 1024),
    )(visible, keep, logit.reshape(1, tokens), queries, keys, values, out_grad)


def per_device(queries, context_keys, context_values, router_logit, keep_index, visible_blocks, out_grad):
    routed_out, query_grad, part = local(
        queries, context_keys, context_values, router_logit, keep_index, visible_blocks, out_grad
    )
    router_grad = lax.psum(part.reshape(-1), "tensor")
    return routed_out, query_grad, router_grad


def solution(mesh):
    return jax.shard_map(
        per_device,
        mesh=mesh,
        in_specs=(
            P("frame", "tensor"),
            P(None, "tensor"),
            P(None, "tensor"),
            P("frame"),
            P("frame", None),
            P("frame"),
            P("frame", "tensor"),
        ),
        out_specs=(P("frame", "tensor"), P("frame", "tensor"), P("frame")),
        check_vma=False,
    )
```

```python
import jax
import jax.numpy as jnp
from jax import lax
from jax.experimental import pallas as pl
from jax.experimental.pallas import tpu as pltpu
from jax.sharding import PartitionSpec as P

HD = 128
MEM_BLOCK = 128
SCALE = HD ** (-0.5)
LOG2E = 1.4426950408889634
UNIT = 2
FEW_UNITS = 2
ROWS = 256
FEW = 224
AHEAD = 2
MANY_REACH = (4, 5, 6, 7, 8, 9)
FEW_REACH = (2, 8, 9)


def dot(a, b):
    return jnp.dot(a, b, preferred_element_type=jnp.float32)


def dot_nt(a, b):
    return lax.dot_general(a, b, (((1,), (1,)), ((), ())), preferred_element_type=jnp.float32)


def half(a):
    return a.astype(jnp.bfloat16)


def attend(q, g, keys, values, hidden):
    heads = range(len(q))
    scores = [dot_nt(q[h], keys[h]) for h in heads]
    dprob = [dot_nt(g[h], values[h]) for h in heads]
    if hidden is not None:
        scores = [hidden(s) for s in scores]
    top = [jnp.max(scores[h], axis=1, keepdims=True) for h in heads]
    terms = [jnp.exp2((scores[h] - top[h]) * (SCALE * LOG2E)) for h in heads]
    ones = jnp.ones(values[0].shape, values[0].dtype)
    sums = [dot(half(terms[h]), jnp.concatenate([values[h], ones], axis=1)) for h in heads]
    inverse = [1.0 / sums[h][:, HD:] for h in heads]
    mixed = [sums[h][:, :HD] * inverse[h] for h in heads]
    delta = [jnp.sum(g[h].astype(jnp.float32) * mixed[h], axis=1, keepdims=True) for h in heads]
    dscore = [half(terms[h] * (dprob[h] - delta[h])) for h in heads]
    dq = [dot(dscore[h], keys[h]) * (inverse[h] * SCALE) for h in heads]
    return [half(m).astype(jnp.float32) for m in mixed], [half(d) for d in dq]


def kernel(
    visible, keep_hbm, logit_hbm, q_hbm, k_hbm, v_hbm, og_hbm,
    out_hbm, dq_hbm, part,
    keep_scalar, keep, logit, q_all, k_all, v_all, og_all, out_all, dq_all,
    gate, pick, place, acc, small_sem, in_sem, out_sem,
):
    tokens, width = q_all.shape
    unit = UNIT * HD
    groups = width // unit

    def columns(group, units=1):
        return pl.ds(pl.multiple_of(group * unit, unit), units * unit)

    def loads(group):
        cols = columns(group)
        pairs = ((q_hbm, q_all), (k_hbm, k_all), (og_hbm, og_all), (v_hbm, v_all))
        return [
            pltpu.make_async_copy(src.at[:, cols], dst.at[:, cols], in_sem.at[i, group])
            for i, (src, dst) in enumerate(pairs)
        ]

    def stores(group):
        cols = columns(group)
        pairs = ((out_all, out_hbm), (dq_all, dq_hbm))
        return [
            pltpu.make_async_copy(src.at[:, cols], dst.at[:, cols], out_sem.at[i, group])
            for i, (src, dst) in enumerate(pairs)
        ]

    small = [
        pltpu.make_async_copy(src, dst, small_sem.at[i])
        for i, (src, dst) in enumerate(
            ((keep_hbm, keep_scalar), (keep_hbm, keep), (logit_hbm, logit))
        )
    ]
    for copy in small:
        copy.start()
    for group in range(AHEAD):
        for copy in loads(group):
            copy.start()
    for copy in small:
        copy.wait()

    gate_row = jax.nn.sigmoid(logit[...])
    gate[...] = jnp.transpose(jnp.broadcast_to(gate_row, (HD, tokens)))
    acc[...] = jnp.zeros_like(acc)
    shown = visible[0]
    full = keep_scalar[0, tokens - 1] < tokens
    few = keep_scalar[0, FEW] >= tokens
    some = jnp.logical_not(full)
    many = jnp.logical_not(few)

    @pl.when(some)
    def _():
        kept = keep[...]
        token = lax.broadcasted_iota(jnp.int32, (tokens, tokens), 0)
        place[...] = half(jnp.where(token == kept, 1.0, 0.0))
        spread = jnp.transpose(jnp.broadcast_to(kept.astype(jnp.float32), (HD, tokens)))
        lane = lax.broadcasted_iota(jnp.int32, (tokens, HD), 1).astype(jnp.float32)
        own = jnp.zeros((tokens, HD), jnp.float32)
        for start in range(0, tokens, HD):
            hit = jnp.where(spread == lane + float(start), 1.0, 0.0)
            pick[:, start : start + HD] = half(hit)
            own = own + hit * gate_row[:, start : start + HD]
        gate[...] = jnp.broadcast_to(jnp.sum(own, axis=1, keepdims=True), (tokens, HD))

    def sweep(units, body):
        @pl.loop(0, groups // units)
        def _(index):
            first = index * units
            for part_of in range(units):
                for copy in loads(first + part_of):
                    copy.wait()

            @pl.when(first + AHEAD < groups)
            def _():
                for part_of in range(units):
                    for copy in loads(first + AHEAD + part_of):
                        copy.start()

            body(first)
            for part_of in range(units):
                for copy in stores(first + part_of):
                    copy.start()

    def head_columns(group, units=1):
        return [
            pl.ds(pl.multiple_of(group * unit + h * HD, HD), HD) for h in range(units * UNIT)
        ]

    def hide(span, exact):
        if exact:
            return None

        def hidden(scores):
            col = lax.broadcasted_iota(jnp.int32, scores.shape, 1)
            return jnp.where(col < shown * MEM_BLOCK, scores, -jnp.inf)

        return hidden

    def tile(span, exact, cols, q, og, gates):
        g = [half(gates * o) for o in og]
        attn, dq = attend(
            q, g, [k_all[:span, c] for c in cols], [v_all[:span, c] for c in cols], hide(span, exact)
        )
        inner = og[0] * attn[0]
        for o, a in zip(og[1:], attn[1:]):
            inner = inner + o * a
        return [half(gates * a) for a in attn], dq, inner

    def run_many(span, exact, group):
        wide_cols = columns(group)
        cols = head_columns(group)

        @pl.when(some)
        def _():
            q_all[:, wide_cols] = half(dot(pick[...], q_all[:, wide_cols]))
            og_all[:, wide_cols] = half(dot(pick[...], og_all[:, wide_cols]))

        routed, dq, inner = tile(
            span, exact, cols,
            [q_all[:, c] for c in cols],
            [og_all[:, c].astype(jnp.float32) for c in cols],
            gate[...],
        )
        for h, c in enumerate(cols):
            out_all[:, c] = routed[h]
            dq_all[:, c] = dq[h]
        acc[...] = acc[...] + inner

        @pl.when(some)
        def _():
            out_all[:, wide_cols] = half(dot(place[...], out_all[:, wide_cols]))
            dq_all[:, wide_cols] = half(dot(place[...], dq_all[:, wide_cols]))

    def run_few(span, exact, group):
        wide_cols = columns(group, FEW_UNITS)
        cols = head_columns(group, FEW_UNITS)
        chosen = pick[:FEW, :]
        q = half(dot(chosen, q_all[:, wide_cols]))
        og = dot(chosen, og_all[:, wide_cols])
        routed, dq, inner = tile(
            span, exact, cols,
            [q[:, h * HD : (h + 1) * HD] for h in range(len(cols))],
            [og[:, h * HD : (h + 1) * HD] for h in range(len(cols))],
            gate[:FEW, :],
        )
        acc[:FEW, :] = acc[:FEW, :] + inner
        blank = jnp.zeros((ROWS - FEW, FEW_UNITS * unit), jnp.bfloat16)
        for target, rows in ((out_all, routed), (dq_all, dq)):
            stacked = jnp.concatenate([jnp.concatenate(rows, axis=1), blank], axis=0)
            target[:, wide_cols] = half(dot(place[:, :ROWS], stacked))

    def choose(reaches, run, units):
        reach, low = reaches[-1], (0, *reaches)[-2]
        span, exact = reach * MEM_BLOCK, reach == low + 1

        def here():
            sweep(units, lambda group: run(span, exact, group))

        if low:
            lax.cond(shown > low, here, lambda: choose(reaches[:-1], run, units))
        else:
            here()

    lax.cond(
        few,
        lambda: choose(FEW_REACH, run_few, FEW_UNITS),
        lambda: choose(MANY_REACH, run_many, 1),
    )

    weight = gate_row * (1.0 - gate_row)

    @pl.when(full)
    def _():
        part[...] = jnp.sum(jnp.transpose(acc[...]), axis=0, keepdims=True) * weight

    @pl.when(some)
    def _():
        inner = jnp.sum(acc[...], axis=1, keepdims=True)
        part[...] = jnp.sum(pick[...].astype(jnp.float32) * inner, axis=0, keepdims=True) * weight

    for group in range(groups):
        for copy in stores(group):
            copy.wait()


def local(queries, keys, values, logit, keep, visible, out_grad):
    tokens, width = queries.shape
    ctx = keys.shape[0]
    groups = width // (UNIT * HD)
    hbm = pl.BlockSpec(memory_space=pltpu.HBM)
    return pl.pallas_call(
        kernel,
        in_specs=[pl.BlockSpec(memory_space=pltpu.SMEM)] + [hbm] * 6,
        out_specs=[hbm, hbm, pl.BlockSpec(memory_space=pltpu.VMEM)],
        out_shape=[
            jax.ShapeDtypeStruct((tokens, width), jnp.bfloat16),
            jax.ShapeDtypeStruct((tokens, width), jnp.bfloat16),
            pltpu.VMEM((1, tokens), jnp.float32),
        ],
        scratch_shapes=[
            pltpu.SMEM((1, tokens), jnp.int32),
            pltpu.VMEM((1, tokens), jnp.int32),
            pltpu.VMEM((1, tokens), jnp.float32),
            pltpu.VMEM((tokens, width), jnp.bfloat16),
            pltpu.VMEM((ctx, width), jnp.bfloat16),
            pltpu.VMEM((ctx, width), jnp.bfloat16),
            pltpu.VMEM((tokens, width), jnp.bfloat16),
            pltpu.VMEM((tokens, width), jnp.bfloat16),
            pltpu.VMEM((tokens, width), jnp.bfloat16),
            pltpu.VMEM((tokens, HD), jnp.float32),
            pltpu.VMEM((tokens, tokens), jnp.bfloat16),
            pltpu.VMEM((tokens, tokens), jnp.bfloat16),
            pltpu.VMEM((tokens, HD), jnp.float32),
            pltpu.SemaphoreType.DMA((3,)),
            pltpu.SemaphoreType.DMA((4, groups)),
            pltpu.SemaphoreType.DMA((2, groups)),
        ],
        compiler_params=pltpu.CompilerParams(vmem_limit_bytes=60 * 1024 * 1024),
    )(visible, keep, logit.reshape(1, tokens), queries, keys, values, out_grad)


def exchange(mine, total, theirs, send, recv):
    peer = {"tensor": 1 - lax.axis_index("tensor")}
    barrier = pltpu.get_barrier_semaphore()
    pl.semaphore_signal(barrier, inc=1, device_id=peer, device_id_type=pl.DeviceIdType.MESH)
    pl.semaphore_wait(barrier, 1)
    copy = pltpu.make_async_remote_copy(
        mine, theirs, send, recv, device_id=peer, device_id_type=pl.DeviceIdType.MESH
    )
    copy.start()
    copy.wait()
    total[...] = mine[...] + theirs[...]


def add_cores(part):
    vmem = pl.BlockSpec(memory_space=pltpu.VMEM)
    return pl.pallas_call(
        exchange,
        in_specs=[vmem],
        out_specs=vmem,
        out_shape=pltpu.VMEM(part.shape, part.dtype),
        scratch_shapes=[
            pltpu.VMEM(part.shape, part.dtype),
            pltpu.SemaphoreType.DMA,
            pltpu.SemaphoreType.DMA,
        ],
        compiler_params=pltpu.CompilerParams(collective_id=0, has_side_effects=True),
    )(pltpu.with_memory_space_constraint(part, pltpu.VMEM))


def per_device(queries, context_keys, context_values, router_logit, keep_index, visible_blocks, out_grad):
    routed_out, query_grad, part = local(
        queries, context_keys, context_values, router_logit, keep_index, visible_blocks, out_grad
    )
    return routed_out, query_grad, add_cores(part).reshape(-1)


def solution(mesh):
    return jax.shard_map(
        per_device,
        mesh=mesh,
        in_specs=(
            P("frame", "tensor"),
            P(None, "tensor"),
            P(None, "tensor"),
            P("frame"),
            P("frame", None),
            P("frame"),
            P("frame", "tensor"),
        ),
        out_specs=(P("frame", "tensor"), P("frame", "tensor"), P("frame")),
        check_vma=False,
    )
```

```python
import jax
import jax.numpy as jnp
from jax import lax
from jax.experimental import pallas as pl
from jax.experimental.pallas import tpu as pltpu
from jax.sharding import PartitionSpec as P

HD = 128
MEM_BLOCK = 128
SCALE = HD ** (-0.5)
LOG2E = 1.4426950408889634
UNIT = 2
FEW_UNITS = 2
ROWS = 256
FEW = 224
AHEAD = 2
MANY_REACH = (4, 5, 6, 7, 8, 9)
FEW_REACH = (2, 8, 9)


def dot(a, b):
    return jnp.dot(a, b, preferred_element_type=jnp.float32)


def dot_nt(a, b):
    return lax.dot_general(a, b, (((1,), (1,)), ((), ())), preferred_element_type=jnp.float32)


def half(a):
    return a.astype(jnp.bfloat16)


def attend(q, g, keys, values, hidden):
    heads = range(len(q))
    scores = [dot_nt(q[h], keys[h]) for h in heads]
    dprob = [dot_nt(g[h], values[h]) for h in heads]
    if hidden is not None:
        scores = [hidden(s) for s in scores]
    top = [jnp.max(scores[h], axis=1, keepdims=True) for h in heads]
    terms = [jnp.exp2((scores[h] - top[h]) * (SCALE * LOG2E)) for h in heads]
    ones = jnp.ones(values[0].shape, values[0].dtype)
    sums = [dot(half(terms[h]), jnp.concatenate([values[h], ones], axis=1)) for h in heads]
    inverse = [1.0 / sums[h][:, HD:] for h in heads]
    mixed = [sums[h][:, :HD] * inverse[h] for h in heads]
    delta = [jnp.sum(g[h].astype(jnp.float32) * mixed[h], axis=1, keepdims=True) for h in heads]
    dscore = [half(terms[h] * (dprob[h] - delta[h])) for h in heads]
    dq = [dot(dscore[h], keys[h]) * (inverse[h] * SCALE) for h in heads]
    return [half(m).astype(jnp.float32) for m in mixed], [half(d) for d in dq]


def kernel(
    visible, keep_hbm, logit_hbm, q_hbm, k_hbm, v_hbm, og_hbm,
    out_hbm, dq_hbm, part,
    keep_scalar, keep, logit, q_all, k_all, v_all, og_all, out_all, dq_all,
    gate, pick, place, acc, small_sem, in_sem, out_sem,
):
    tokens, width = q_all.shape
    unit = UNIT * HD
    groups = width // unit

    def columns(group, units=1):
        return pl.ds(pl.multiple_of(group * unit, unit), units * unit)

    def loads(group):
        cols = columns(group)
        pairs = ((q_hbm, q_all), (k_hbm, k_all), (og_hbm, og_all), (v_hbm, v_all))
        return [
            pltpu.make_async_copy(src.at[:, cols], dst.at[:, cols], in_sem.at[i, group])
            for i, (src, dst) in enumerate(pairs)
        ]

    def stores(group):
        cols = columns(group)
        pairs = ((out_all, out_hbm), (dq_all, dq_hbm))
        return [
            pltpu.make_async_copy(src.at[:, cols], dst.at[:, cols], out_sem.at[i, group])
            for i, (src, dst) in enumerate(pairs)
        ]

    small = [
        pltpu.make_async_copy(src, dst, small_sem.at[i])
        for i, (src, dst) in enumerate(
            ((keep_hbm, keep_scalar), (keep_hbm, keep), (logit_hbm, logit))
        )
    ]
    for copy in small:
        copy.start()
    for copy in loads(0):
        copy.start()
    for copy in small:
        copy.wait()
    for group in range(1, AHEAD):
        for copy in loads(group):
            copy.start()

    gate_row = jax.nn.sigmoid(logit[...])
    gate[...] = jnp.transpose(jnp.broadcast_to(gate_row, (HD, tokens)))
    acc[...] = jnp.zeros_like(acc)
    shown = visible[0]
    full = keep_scalar[0, tokens - 1] < tokens
    few = keep_scalar[0, FEW] >= tokens
    some = jnp.logical_not(full)
    many = jnp.logical_not(few)

    @pl.when(some)
    def _():
        kept = keep[...]
        token = lax.broadcasted_iota(jnp.int32, (tokens, tokens), 0)
        place[...] = half(jnp.where(token == kept, 1.0, 0.0))
        spread = jnp.transpose(jnp.broadcast_to(kept.astype(jnp.float32), (HD, tokens)))
        lane = lax.broadcasted_iota(jnp.int32, (tokens, HD), 1).astype(jnp.float32)
        own = jnp.zeros((tokens, HD), jnp.float32)
        for start in range(0, tokens, HD):
            hit = jnp.where(spread == lane + float(start), 1.0, 0.0)
            pick[:, start : start + HD] = half(hit)
            own = own + hit * gate_row[:, start : start + HD]
        gate[...] = jnp.broadcast_to(jnp.sum(own, axis=1, keepdims=True), (tokens, HD))

    def sweep(units, body):
        @pl.loop(0, groups // units)
        def _(index):
            first = index * units
            for part_of in range(units):
                for copy in loads(first + part_of):
                    copy.wait()

            @pl.when(first + AHEAD < groups)
            def _():
                for part_of in range(units):
                    for copy in loads(first + AHEAD + part_of):
                        copy.start()

            body(first)
            for part_of in range(units):
                for copy in stores(first + part_of):
                    copy.start()

    def head_columns(group, units=1):
        return [
            pl.ds(pl.multiple_of(group * unit + h * HD, HD), HD) for h in range(units * UNIT)
        ]

    def hide(span, exact):
        if exact:
            return None

        def hidden(scores):
            col = lax.broadcasted_iota(jnp.int32, scores.shape, 1)
            return jnp.where(col < shown * MEM_BLOCK, scores, -jnp.inf)

        return hidden

    def tile(span, exact, cols, q, og, gates):
        g = [half(gates * o) for o in og]
        attn, dq = attend(
            q, g, [k_all[:span, c] for c in cols], [v_all[:span, c] for c in cols], hide(span, exact)
        )
        inner = og[0] * attn[0]
        for o, a in zip(og[1:], attn[1:]):
            inner = inner + o * a
        return [half(gates * a) for a in attn], dq, inner

    def run_many(span, exact, group):
        wide_cols = columns(group)
        cols = head_columns(group)

        @pl.when(some)
        def _():
            q_all[:, wide_cols] = half(dot(pick[...], q_all[:, wide_cols]))
            og_all[:, wide_cols] = half(dot(pick[...], og_all[:, wide_cols]))

        routed, dq, inner = tile(
            span, exact, cols,
            [q_all[:, c] for c in cols],
            [og_all[:, c].astype(jnp.float32) for c in cols],
            gate[...],
        )
        for h, c in enumerate(cols):
            out_all[:, c] = routed[h]
            dq_all[:, c] = dq[h]
        acc[...] = acc[...] + inner

        @pl.when(some)
        def _():
            out_all[:, wide_cols] = half(dot(place[...], out_all[:, wide_cols]))
            dq_all[:, wide_cols] = half(dot(place[...], dq_all[:, wide_cols]))

    def run_few(span, exact, group):
        wide_cols = columns(group, FEW_UNITS)
        cols = head_columns(group, FEW_UNITS)
        chosen = pick[:FEW, :]
        q = half(dot(chosen, q_all[:, wide_cols]))
        og = dot(chosen, og_all[:, wide_cols])
        routed, dq, inner = tile(
            span, exact, cols,
            [q[:, h * HD : (h + 1) * HD] for h in range(len(cols))],
            [og[:, h * HD : (h + 1) * HD] for h in range(len(cols))],
            gate[:FEW, :],
        )
        acc[:FEW, :] = acc[:FEW, :] + inner
        blank = jnp.zeros((ROWS - FEW, FEW_UNITS * unit), jnp.bfloat16)
        for target, rows in ((out_all, routed), (dq_all, dq)):
            stacked = jnp.concatenate([jnp.concatenate(rows, axis=1), blank], axis=0)
            target[:, wide_cols] = half(dot(place[:, :ROWS], stacked))

    def choose(reaches, run, units):
        reach, low = reaches[-1], (0, *reaches)[-2]
        span, exact = reach * MEM_BLOCK, reach == low + 1

        def here():
            sweep(units, lambda group: run(span, exact, group))

        if low:
            lax.cond(shown > low, here, lambda: choose(reaches[:-1], run, units))
        else:
            here()

    lax.cond(
        few,
        lambda: choose(FEW_REACH, run_few, FEW_UNITS),
        lambda: choose(MANY_REACH, run_many, 1),
    )

    weight = gate_row * (1.0 - gate_row)

    @pl.when(full)
    def _():
        part[...] = jnp.sum(jnp.transpose(acc[...]), axis=0, keepdims=True) * weight

    @pl.when(some)
    def _():
        inner = jnp.sum(acc[...], axis=1, keepdims=True)
        part[...] = jnp.sum(pick[...].astype(jnp.float32) * inner, axis=0, keepdims=True) * weight

    for group in range(groups):
        for copy in stores(group):
            copy.wait()


def local(queries, keys, values, logit, keep, visible, out_grad):
    tokens, width = queries.shape
    ctx = keys.shape[0]
    groups = width // (UNIT * HD)
    hbm = pl.BlockSpec(memory_space=pltpu.HBM)
    return pl.pallas_call(
        kernel,
        in_specs=[pl.BlockSpec(memory_space=pltpu.SMEM)] + [hbm] * 6,
        out_specs=[hbm, hbm, pl.BlockSpec(memory_space=pltpu.VMEM)],
        out_shape=[
            jax.ShapeDtypeStruct((tokens, width), jnp.bfloat16),
            jax.ShapeDtypeStruct((tokens, width), jnp.bfloat16),
            pltpu.VMEM((1, tokens), jnp.float32),
        ],
        scratch_shapes=[
            pltpu.SMEM((1, tokens), jnp.int32),
            pltpu.VMEM((1, tokens), jnp.int32),
            pltpu.VMEM((1, tokens), jnp.float32),
            pltpu.VMEM((tokens, width), jnp.bfloat16),
            pltpu.VMEM((ctx, width), jnp.bfloat16),
            pltpu.VMEM((ctx, width), jnp.bfloat16),
            pltpu.VMEM((tokens, width), jnp.bfloat16),
            pltpu.VMEM((tokens, width), jnp.bfloat16),
            pltpu.VMEM((tokens, width), jnp.bfloat16),
            pltpu.VMEM((tokens, HD), jnp.float32),
            pltpu.VMEM((tokens, tokens), jnp.bfloat16),
            pltpu.VMEM((tokens, tokens), jnp.bfloat16),
            pltpu.VMEM((tokens, HD), jnp.float32),
            pltpu.SemaphoreType.DMA((3,)),
            pltpu.SemaphoreType.DMA((4, groups)),
            pltpu.SemaphoreType.DMA((2, groups)),
        ],
        compiler_params=pltpu.CompilerParams(vmem_limit_bytes=60 * 1024 * 1024),
    )(visible, keep, logit.reshape(1, tokens), queries, keys, values, out_grad)


def exchange(mine, total, theirs, send, recv):
    peer = {"tensor": 1 - lax.axis_index("tensor")}
    barrier = pltpu.get_barrier_semaphore()
    pl.semaphore_signal(barrier, inc=1, device_id=peer, device_id_type=pl.DeviceIdType.MESH)
    pl.semaphore_wait(barrier, 1)
    copy = pltpu.make_async_remote_copy(
        mine, theirs, send, recv, device_id=peer, device_id_type=pl.DeviceIdType.MESH
    )
    copy.start()
    copy.wait()
    total[...] = mine[...] + theirs[...]


def add_cores(part):
    vmem = pl.BlockSpec(memory_space=pltpu.VMEM)
    return pl.pallas_call(
        exchange,
        in_specs=[vmem],
        out_specs=vmem,
        out_shape=pltpu.VMEM(part.shape, part.dtype),
        scratch_shapes=[
            pltpu.VMEM(part.shape, part.dtype),
            pltpu.SemaphoreType.DMA,
            pltpu.SemaphoreType.DMA,
        ],
        compiler_params=pltpu.CompilerParams(collective_id=0, has_side_effects=True),
    )(pltpu.with_memory_space_constraint(part, pltpu.VMEM))


def per_device(queries, context_keys, context_values, router_logit, keep_index, visible_blocks, out_grad):
    routed_out, query_grad, part = local(
        queries, context_keys, context_values, router_logit, keep_index, visible_blocks, out_grad
    )
    return routed_out, query_grad, add_cores(part).reshape(-1)


def solution(mesh):
    return jax.shard_map(
        per_device,
        mesh=mesh,
        in_specs=(
            P("frame", "tensor"),
            P(None, "tensor"),
            P(None, "tensor"),
            P("frame"),
            P("frame", None),
            P("frame"),
            P("frame", "tensor"),
        ),
        out_specs=(P("frame", "tensor"), P("frame", "tensor"), P("frame")),
        check_vma=False,
    )
```
